32 devices in a mesh: seq: 8 (over z, x), tp: 4 (over y, core).
Axes of the slice: x: 2, y: 2, z: 4, core: 2. Of those that a mesh axis runs over, the one named last changes fastest.
Arguments:
- queries: bfloat16 [40, 1536], P(None, 'tp'), may hold values from -6 to 6
- new_keys: bfloat16 [40, 512], P('seq', 'tp'), may hold values from -12 to 12
- new_values: bfloat16 [40, 512], P('seq', 'tp'), may hold values from -6 to 6
- key_cache: bfloat16 [65536, 512], P('seq', 'tp'), may hold values from -64 to 64
- value_cache: bfloat16 [65536, 512], P('seq', 'tp'), may hold values from -6 to 6
- out_weight: bfloat16 [1536, 1536], P('tp'), may hold values from -0.75 to 0.75
- group_ids: int32 [8], replicated, may hold values from 0 to 2, as said below
- prefix_len: int32 [3], replicated, may hold values from 2560 to 10240, as said below
- suffix_len: int32 [8], replicated, may hold values from 1536 to 6144, as said below
Outputs:
- attended: bfloat16 [40, 1536], P('seq', 'tp')
The draws below stay inside these ranges and needn't reach their ends.
Inputs may be any that keep to these rules, and one draw needn't show every extreme that they name: `group_ids`: non-decreasing; every prompt is used by 2 to 4 requests. `prefix_len`: some prompt has exactly 10240 positions. `suffix_len`: some request has exactly 6144 own positions.
All inputs are finite; a program needn't handle non-finite values.
Results may differ from the reference program's by a relative error of at most 0.011.
Values sent between devices are 32-bit elements; how exact they have to be, the bound alone decides.
A program may use at most 64 MiB of HBM per device.

```python
import jax
import jax.numpy as jnp
from jax import lax

H = 24
KVH = 8
HD = 64
D = 1536
NEW = 5
REQ = 8
GROUPS = 3
GMIN = 2
ROWS = 40
CACHE = 65536
PRE_MAX = 10240
SUF_MAX = 6144


def layout(key):
    inner = jax.random.fold_in(key, 101)
    key_a, key_b, key_c, key_d, key_e = jax.random.split(inner, 5)
    groups = jnp.arange(GROUPS, dtype=jnp.int32)
    slots = jax.random.permutation(key_a, GROUPS * GMIN).astype(jnp.int32)
    chosen = (slots[:REQ - GMIN * GROUPS] // GMIN).astype(jnp.int32)
    sizes = (GMIN + jnp.sum((chosen[:, None] == groups[None, :]).astype(jnp.int32), axis=0)).astype(jnp.int32)
    ends = jnp.cumsum(sizes).astype(jnp.int32)
    index = jnp.arange(REQ, dtype=jnp.int32)
    group_ids = jnp.sum((index[:, None] >= ends[None, :]).astype(jnp.int32), axis=1).astype(jnp.int32)
    prefix = jax.random.randint(key_b, (GROUPS,), PRE_MAX // 4, PRE_MAX + 1, dtype=jnp.int32)
    widest = jax.random.randint(key_c, (), 0, GROUPS, dtype=jnp.int32)
    prefix = jnp.where(groups == widest, PRE_MAX, prefix).astype(jnp.int32)
    suffix = jax.random.randint(key_d, (REQ,), SUF_MAX // 4, SUF_MAX + 1, dtype=jnp.int32)
    longest = jax.random.randint(key_e, (), 0, REQ, dtype=jnp.int32)
    suffix = jnp.where(index == longest, SUF_MAX, suffix).astype(jnp.int32)
    return (group_ids, prefix, suffix)


def draw_group_ids(key, part):
    return layout(key)[0]


def draw_prefix_len(key, part):
    return layout(key)[1]


def draw_suffix_len(key, part):
    return layout(key)[2]


def float_base(key, salt, shape):
    inner = jax.random.fold_in(key, salt)
    values = jnp.clip(jax.random.normal(inner, shape, jnp.float32), -6.0, 6.0)
    return values


def draw_queries(key, part):
    return float_base(key, 202, (ROWS, H * HD)).astype(jnp.bfloat16)


def draw_new_keys(key, part):
    query = float_base(key, 202, (ROWS, H * HD)).reshape(ROWS, KVH, H // KVH, HD)
    noise = float_base(key, 303, (ROWS, KVH, HD))
    keys = 0.5 * jnp.sum(query, axis=2) + 0.5 * noise
    return keys.reshape(ROWS, KVH * HD).astype(jnp.bfloat16)


def draw_key_cache(key, part):
    cache = float_base(key, 404, (CACHE, KVH * HD))
    return cache.astype(jnp.bfloat16)


def block_levels(stream_key, dims, cuts, low, high):
    gain = 1.0
    for axis_at, parts in cuts:
        steps = jax.random.uniform(jax.random.fold_in(jax.random.fold_in(stream_key, 6), axis_at), (parts,), jnp.float32, low / len(cuts), high / len(cuts))
        gain = gain * jnp.repeat(jnp.exp(steps), dims[axis_at] // parts).reshape((-1,) + (1,) * (len(dims) - 1 - axis_at))
    return gain


def centred(key, extent, deviation, limit, pieces=(), held_as=jnp.bfloat16):
    gain = block_levels(key, extent, pieces, -0.22, 0.18) if pieces else 1.0
    entries = jax.random.normal(key, extent, jnp.float32) * deviation * gain
    return jnp.minimum(jnp.maximum(entries, -limit), limit).astype(held_as)


def setup_inputs(seed: int = 0) -> dict:
    arg_keys = jax.random.split(jax.random.key(seed), 10)
    return {
        "queries": draw_queries(jax.random.fold_in(arg_keys[9], 71), 0),
        "new_keys": draw_new_keys(jax.random.fold_in(arg_keys[9], 71), 0),
        "new_values": centred(arg_keys[2], (ROWS, KVH * HD), 1.0, 6.0, ((0, 8), (1, 4))),
        "key_cache": draw_key_cache(jax.random.fold_in(arg_keys[9], 71), 0),
        "value_cache": centred(arg_keys[4], (CACHE, KVH * HD), 1.0, 6.0, ((0, 8), (1, 4))),
        "out_weight": centred(arg_keys[5], (H * HD, D), HD ** -0.5, 0.75, ((0, 4),)),
        "group_ids": draw_group_ids(jax.random.fold_in(arg_keys[9], 71), 0),
        "prefix_len": draw_prefix_len(jax.random.fold_in(arg_keys[9], 71), 0),
        "suffix_len": draw_suffix_len(jax.random.fold_in(arg_keys[9], 71), 0),
    }


fill_score = -1e30


def segment_starts(group_ids, prefix_len, suffix_len):
    groups = jnp.arange(prefix_len.shape[0], dtype=jnp.int32)
    prefix_excl = (jnp.cumsum(prefix_len) - prefix_len).astype(jnp.int32)
    suffix_excl = (jnp.cumsum(suffix_len) - suffix_len).astype(jnp.int32)
    earlier = group_ids[None, :] < groups[:, None]
    prompt_start = prefix_excl + jnp.sum(jnp.where(earlier, suffix_len[None, :], 0), axis=1).astype(jnp.int32)
    member = group_ids[:, None] == groups[None, :]
    req_prompt_start = jnp.sum(jnp.where(member, prompt_start[None, :], 0), axis=1).astype(jnp.int32)
    req_prompt_len = jnp.sum(jnp.where(member, prefix_len[None, :], 0), axis=1).astype(jnp.int32)
    prefix_incl = jnp.sum(jnp.where(member, (prefix_excl + prefix_len)[None, :], 0), axis=1).astype(jnp.int32)
    own_start = (prefix_incl + suffix_excl).astype(jnp.int32)
    return req_prompt_start, req_prompt_len, own_start


def reference(queries, new_keys, new_values, key_cache, value_cache, out_weight, group_ids, prefix_len, suffix_len):
    prompt_start, prompt_len, own_start = segment_starts(group_ids, prefix_len, suffix_len)
    rep = H // KVH
    query_all = queries.reshape(REQ, NEW, KVH, rep, HD)
    keys_new = new_keys.reshape(REQ, NEW, KVH, HD)
    values_new = new_values.reshape(REQ, NEW, KVH, HD)
    causal = jnp.arange(NEW)[:, None] >= jnp.arange(NEW)[None, :]

    def one_request(index):
        pstart = jnp.minimum(prompt_start[index], CACHE - PRE_MAX).astype(jnp.int32)
        sstart = jnp.minimum(own_start[index], CACHE - SUF_MAX).astype(jnp.int32)
        keys_p = lax.dynamic_slice_in_dim(key_cache, pstart, PRE_MAX, 0)
        vals_p = lax.dynamic_slice_in_dim(value_cache, pstart, PRE_MAX, 0)
        keys_s = lax.dynamic_slice_in_dim(key_cache, sstart, SUF_MAX, 0)
        vals_s = lax.dynamic_slice_in_dim(value_cache, sstart, SUF_MAX, 0)
        pos_p = pstart + jnp.arange(PRE_MAX, dtype=jnp.int32)
        pos_s = sstart + jnp.arange(SUF_MAX, dtype=jnp.int32)
        live_p = (pos_p >= prompt_start[index]) & (pos_p < prompt_start[index] + prompt_len[index])
        live_s = (pos_s >= own_start[index]) & (pos_s < own_start[index] + suffix_len[index])
        cached = jnp.concatenate([live_p, live_s])
        live = jnp.concatenate([jnp.broadcast_to(cached[None, :], (NEW, cached.shape[0])), causal], axis=1)
        keys = jnp.concatenate([keys_p.reshape(PRE_MAX, KVH, HD), keys_s.reshape(SUF_MAX, KVH, HD), keys_new[index]], axis=0)
        vals = jnp.concatenate([vals_p.reshape(PRE_MAX, KVH, HD), vals_s.reshape(SUF_MAX, KVH, HD), values_new[index]], axis=0)
        score = jnp.einsum("tgjd,lgd->tgjl", query_all[index].astype(jnp.float32), keys.astype(jnp.float32)) * 0.125
        mask = live[:, None, None, :]
        score = jnp.where(mask, score, fill_score)
        top = jnp.max(score, axis=-1, keepdims=True)
        expo = jnp.where(mask, jnp.exp(score - top), 0.0)
        total = jnp.sum(expo, axis=-1)
        weight = lax.optimization_barrier(expo.astype(jnp.bfloat16)).astype(jnp.float32)
        summed = jnp.einsum("tgjl,lgd->tgjd", weight, vals.astype(jnp.float32))
        return (summed / total[..., None]).astype(jnp.bfloat16).reshape(NEW, H * HD)

    mixed = lax.map(one_request, jnp.arange(REQ, dtype=jnp.int32)).reshape(ROWS, H * HD)
    return jnp.dot(mixed, out_weight, preferred_element_type=jnp.float32).astype(jnp.bfloat16)
```

```python
import functools

import jax
import jax.numpy as jnp
from jax import lax
from jax.experimental import pallas as pl
from jax.experimental.pallas import tpu as pltpu
from jax.sharding import PartitionSpec as P

HD = 64
NEW = 5
CHUNK = 1024
ROWS_REQ = 32
HALF = 16
MASKED = -1e30
FLOOR = -1e29
MESH = pl.DeviceIdType.MESH


def nt_dot(a, b):
    return lax.dot_general(a, b, (((1,), (1,)), ((), ())), preferred_element_type=jnp.float32)


def pack_halves(x, lane_low):
    parts = []
    for i in range(x.shape[0] // ROWS_REQ):
        first = x[i * ROWS_REQ : i * ROWS_REQ + HALF]
        second = x[i * ROWS_REQ + HALF : (i + 1) * ROWS_REQ]
        parts.append(jnp.where(lane_low, first, second))
    return parts[0] if len(parts) == 1 else jnp.concatenate(parts, axis=0)


def kernel(
    n_seq,
    n_tp,
    window,
    gid_ref,
    plen_ref,
    slen_ref,
    q_ref,
    nk_ref,
    nv_ref,
    k_hbm,
    v_hbm,
    w_hbm,
    out_ref,
    kbuf,
    vbuf,
    wbuf,
    qbuf,
    newbuf,
    mbuf,
    lbuf,
    abuf,
    sendbuf,
    recvbuf,
    mixbuf,
    psend,
    precv,
    k_sem,
    v_sem,
    w_sem,
    send_sem,
    recv_sem,
    psend_sem,
    precv_sem,
):
    me = lax.axis_index("seq")
    mine = lax.axis_index("tp")
    requests = gid_ref.shape[0]
    groups = plen_ref.shape[0]
    block = kbuf.shape[0]
    chunks = block // CHUNK
    heads = q_ref.shape[1] // HD
    rep = heads // 2

    k_copies, v_copies = [], []
    for c in range(chunks):
        rows = pl.ds(c * CHUNK, CHUNK)
        kc = pltpu.make_async_copy(k_hbm.at[rows], kbuf.at[rows], k_sem.at[c])
        vc = pltpu.make_async_copy(v_hbm.at[rows], vbuf.at[rows], v_sem.at[c])
        kc.start()
        vc.start()
        k_copies.append(kc)
        v_copies.append(vc)
    w_copies = []
    for j in range(rep):
        for g in range(2):
            wc = pltpu.make_async_copy(
                w_hbm.at[pl.ds((g * rep + j) * HD, HD)],
                wbuf.at[pl.ds((j * 2 + g) * HD, HD)],
                w_sem.at[j * 2 + g],
            )
            wc.start()
            w_copies.append(wc)

    barrier = pltpu.get_barrier_semaphore()
    for k in range(1, n_seq):
        pl.semaphore_signal(
            barrier, inc=1, device_id={"seq": lax.rem(me + k, n_seq)}, device_id_type=MESH
        )
    for k in range(1, n_tp):
        pl.semaphore_signal(
            barrier, inc=1, device_id={"tp": lax.rem(mine + k, n_tp)}, device_id_type=MESH
        )

    run = jnp.int32(0)
    base = jnp.int32(0)
    before = None
    spans = []
    for r in range(requests):
        g = gid_ref[r]
        if r > 0:
            base = jnp.where(g != before, run, base)
        before = g
        earlier = jnp.int32(0)
        here = jnp.int32(0)
        for i in range(groups):
            length = plen_ref[i]
            earlier = earlier + jnp.where(g > i, length, 0)
            here = jnp.where(g == i, length, here)
        own = slen_ref[r]
        spans.append((earlier + base, here, earlier + here + run, own))
        run = run + own

    span = 8 * NEW
    row = lax.broadcasted_iota(jnp.int32, (8 * ROWS_REQ, span), 0)
    col = lax.broadcasted_iota(jnp.int32, (8 * ROWS_REQ, span), 1)
    place = row & (HALF - 1)
    rrep = sum((place >= NEW * j).astype(jnp.int32) for j in range(1, rep))
    head = ((row >> 4) & 1) * rep + rrep
    match = (col == (row >> 5) * NEW + place - NEW * rrep) & (place < rep * NEW)
    same = (head & 1) == ((row >> 4) & 1)
    lane = lax.broadcasted_iota(jnp.int32, (8 * ROWS_REQ, 2 * HD), 1)
    group_row = (lax.broadcasted_iota(jnp.int32, (8 * ROWS_REQ, 2 * HD), 0) >> 4) & 1
    in_group = (lane >= HD).astype(jnp.int32) == group_row
    straight = []
    crossed = []
    for tile in range(heads // 2):
        at = match & ((head >> 1) == tile)
        straight.append((at & same).astype(jnp.float32).astype(jnp.bfloat16))
        crossed.append((at & ~same).astype(jnp.float32).astype(jnp.bfloat16))
    q_all = q_ref[...]
    for i in range(requests // 8):
        keep = jnp.zeros((8 * ROWS_REQ, 2 * HD), jnp.float32)
        turn = jnp.zeros((8 * ROWS_REQ, 2 * HD), jnp.float32)
        for tile in range(heads // 2):
            piece = q_all[i * span : (i + 1) * span, tile * 2 * HD : (tile + 1) * 2 * HD]
            keep += jnp.dot(straight[tile], piece, preferred_element_type=jnp.float32)
            turn += jnp.dot(crossed[tile], piece, preferred_element_type=jnp.float32)
        both = (keep + pltpu.roll(turn, HD, 1)) * 0.125
        both = jnp.where(in_group, both, 0.0)
        qbuf[pl.ds(i * 8 * ROWS_REQ, 8 * ROWS_REQ), :] = both.astype(jnp.bfloat16)

    lane_low = lax.broadcasted_iota(jnp.int32, (HALF, 2 * HD), 1) < HD

    newbuf[...] = jnp.zeros_like(newbuf)
    newbuf[0, 0:NEW, :] = nk_ref[...].astype(jnp.float32)
    newbuf[1, 0:NEW, :] = nv_ref[...].astype(jnp.float32)
    q_own = qbuf[pl.ds(pl.multiple_of(me * ROWS_REQ, ROWS_REQ), ROWS_REQ), :]
    s_new = nt_dot(q_own, newbuf[0].astype(jnp.bfloat16))
    place_n = lax.broadcasted_iota(jnp.int32, s_new.shape, 0) & (HALF - 1)
    token_n = place_n - sum(
        (place_n >= NEW * j).astype(jnp.int32) * NEW for j in range(1, rep + 1)
    )
    causal = lax.broadcasted_iota(jnp.int32, s_new.shape, 1) <= token_n
    s_new = jnp.where(causal, s_new, MASKED)
    m_new = jnp.max(s_new, axis=1, keepdims=True)
    p_new = jnp.exp(s_new - m_new)
    l_new = jnp.sum(p_new, axis=1, keepdims=True)
    a_new = jnp.dot(
        p_new.astype(jnp.bfloat16),
        newbuf[1].astype(jnp.bfloat16),
        preferred_element_type=jnp.float32,
    )
    o_new = pack_halves(a_new / l_new, lane_low)
    stat_new = pack_halves(m_new + jnp.log(l_new), lane_low)

    offset = me * block
    wpad = -(-window // 8) * 8
    slot = lax.broadcasted_iota(jnp.int32, (wpad, 128), 0)
    pos = lax.broadcasted_iota(jnp.int32, (wpad, CHUNK), 1)
    bounds = []
    for f in range(4):
        vec = jnp.zeros((wpad, 128), jnp.int32)
        for i in range(window):
            vec = jnp.where(slot == i, spans[i][f], vec)
        bounds.append(vec[:, 0:1])
    for c in range(chunks):
        start = offset + c * CHUNK
        shifted = pos + start
        from_p = shifted - bounds[0]
        from_o = shifted - bounds[2]
        live = ((from_p >= 0) & (from_p < bounds[1])) | ((from_o >= 0) & (from_o < bounds[3]))
        bias = jnp.where(live, 0.0, MASKED)

        k_copies[c].wait()
        s = nt_dot(qbuf[...], kbuf[pl.ds(c * CHUNK, CHUNK), :])
        ps, ms, ls = [], [], []
        for i in range(window):
            si = s[i * ROWS_REQ : (i + 1) * ROWS_REQ] + bias[i : i + 1, :]
            mi = jnp.maximum(jnp.max(si, axis=1, keepdims=True), FLOOR)
            pi = jnp.exp(si - mi)
            ls.append(jnp.sum(pi, axis=1, keepdims=True))
            ms.append(mi)
            ps.append(pi.astype(jnp.bfloat16))
        v_copies[c].wait()
        acc = jnp.dot(
            jnp.concatenate(ps, axis=0),
            vbuf[pl.ds(c * CHUNK, CHUNK), :],
            preferred_element_type=jnp.float32,
        )
        abuf[c] = pack_halves(acc, lane_low)
        for i in range(window):
            at = pl.ds(i * HALF, HALF)
            mbuf[c, at, :] = pack_halves(ms[i], lane_low)
            lbuf[c, at, :] = pack_halves(ls[i], lane_low)

    def merged(r):
        tops, sums, accs = [], [], []
        for c in range(chunks):
            at = pl.ds(pl.multiple_of(r * HALF, HALF), HALF)
            tops.append(mbuf[c, at, :])
            sums.append(lbuf[c, at, :])
            accs.append(abuf[c, at, :])
        top = functools.reduce(jnp.maximum, tops, jnp.full((HALF, 2 * HD), FLOOR, jnp.float32))
        total = jnp.zeros((HALF, 2 * HD), jnp.float32)
        summed = jnp.zeros((HALF, 2 * HD), jnp.float32)
        for m, l, a in zip(tops, sums, accs):
            w = jnp.exp(m - top)
            total += w * l
            summed += w * a
        some = total > 0.0
        safe = jnp.where(some, total, 1.0)
        return summed / safe, jnp.where(some, top + jnp.log(safe), MASKED)

    pl.semaphore_wait(barrier, n_seq - 1 + n_tp - 1)

    def seq_copy(k):
        return pltpu.make_async_remote_copy(
            src_ref=sendbuf.at[k],
            dst_ref=recvbuf.at[k],
            send_sem=send_sem.at[k],
            recv_sem=recv_sem.at[k],
            device_id={"seq": lax.rem(me + k, n_seq)},
            device_id_type=MESH,
        )

    def send_part(k, carry):
        o, stat = merged(lax.rem(me + k, n_seq))
        sendbuf[k, 0:HALF, :] = o
        sendbuf[k, HALF : 2 * HALF, :] = stat
        seq_copy(k).start()
        return carry

    if n_seq <= 8:
        for k in range(1, n_seq):
            send_part(k, 0)
    else:
        lax.fori_loop(1, n_seq, send_part, 0)

    o_here, stat_here = merged(me)

    def take(carry, o, stat):
        top, total, summed = carry
        higher = jnp.maximum(top, stat)
        a, b = jnp.exp(top - higher), jnp.exp(stat - higher)
        return higher, total * a + b, summed * a + o * b

    carry = (stat_new, jnp.ones_like(stat_new), o_new)
    carry = take(carry, o_here, stat_here)
    if n_seq <= 8:
        for k in range(1, n_seq):
            seq_copy(k).wait_recv()
        stats = [recvbuf[k, HALF : 2 * HALF, :] for k in range(1, n_seq)]
        top = functools.reduce(jnp.maximum, stats, carry[0])
        fac = jnp.exp(carry[0] - top)
        total, summed = carry[1] * fac, carry[2] * fac
        for k in range(1, n_seq):
            w = jnp.exp(stats[k - 1] - top)
            total += w
            summed += w * recvbuf[k, 0:HALF, :]
    else:

        def take_part(k, carry):
            seq_copy(k).wait_recv()
            return take(carry, recvbuf[k, 0:HALF, :], recvbuf[k, HALF : 2 * HALF, :])

        _, total, summed = lax.fori_loop(1, n_seq, take_part, carry)
    mixbuf[...] = jnp.zeros_like(mixbuf)
    mixbuf[0:HALF, :] = summed / total
    lhs = jnp.concatenate([mixbuf[pl.ds(NEW * j, 8), :] for j in range(rep)], axis=1)
    lhs = lhs.astype(jnp.bfloat16)
    for wc in w_copies:
        wc.wait()
    partial = jnp.dot(lhs, wbuf[...], preferred_element_type=jnp.float32)
    width = psend.shape[2]
    for i in range(n_tp):
        psend[i] = partial[:, i * width : (i + 1) * width]
    copies = []
    for k in range(1, n_tp):
        dest = lax.rem(mine + k, n_tp)
        pc = pltpu.make_async_remote_copy(
            src_ref=psend.at[dest],
            dst_ref=precv.at[k],
            send_sem=psend_sem.at[k],
            recv_sem=precv_sem.at[k],
            device_id={"tp": dest},
            device_id_type=MESH,
        )
        pc.start()
        copies.append(pc)
    result = psend[mine]
    for k, pc in enumerate(copies, 1):
        pc.wait_recv()
        result = result + precv[k]
    out_ref[...] = result[0:NEW].astype(jnp.bfloat16)
    for pc in copies:
        pc.wait_send()
    if n_seq <= 8:
        for k in range(1, n_seq):
            seq_copy(k).wait_send()
    else:

        def finish(k, carry):
            seq_copy(k).wait_send()
            return carry

        lax.fori_loop(1, n_seq, finish, 0)


def solution(mesh):
    n_seq, n_tp = mesh.shape["seq"], mesh.shape["tp"]

    def per_device(q, nk, nv, kc, vc, w, gid, plen, slen):
        requests, groups = gid.shape[0], plen.shape[0]
        block = kc.shape[0]
        chunks = block // CHUNK
        window = requests
        width = w.shape[1] // n_tp
        smem = pl.BlockSpec(memory_space=pltpu.SMEM)
        vmem = pl.BlockSpec(memory_space=pltpu.VMEM)
        hbm = pl.BlockSpec(memory_space=pl.ANY)
        f32, bf16 = jnp.float32, jnp.bfloat16
        dma = pltpu.SemaphoreType.DMA
        return pl.pallas_call(
            functools.partial(kernel, n_seq, n_tp, window),
            out_shape=jax.ShapeDtypeStruct((NEW, width), bf16),
            in_specs=[smem] * 3 + [vmem] * 3 + [hbm] * 3,
            out_specs=vmem,
            scratch_shapes=[
                pltpu.VMEM((block, 2 * HD), bf16),
                pltpu.VMEM((block, 2 * HD), bf16),
                pltpu.VMEM(w.shape, bf16),
                pltpu.VMEM((requests * ROWS_REQ, 2 * HD), bf16),
                pltpu.VMEM((2, HALF, 2 * HD), f32),
                pltpu.VMEM((chunks, window * HALF, 2 * HD), f32),
                pltpu.VMEM((chunks, window * HALF, 2 * HD), f32),
                pltpu.VMEM((chunks, window * HALF, 2 * HD), f32),
                pltpu.VMEM((n_seq, 2 * HALF, 2 * HD), f32),
                pltpu.VMEM((n_seq, 2 * HALF, 2 * HD), f32),
                pltpu.VMEM((24, 2 * HD), f32),
                pltpu.VMEM((n_tp, 8, width), f32),
                pltpu.VMEM((n_tp, 8, width), f32),
                dma((chunks,)),
                dma((chunks,)),
                dma((w.shape[0] // HD,)),
                dma((n_seq,)),
                dma((n_seq,)),
                dma((n_tp,)),
                dma((n_tp,)),
            ],
            compiler_params=pltpu.CompilerParams(
                collective_id=0, has_side_effects=True, vmem_limit_bytes=48 * 1024 * 1024
            ),
            name="attend",
        )(gid, plen, slen, q, nk, nv, kc, vc, w)

    placed = (
        P(None, "tp"),
        P("seq", "tp"),
        P("seq", "tp"),
        P("seq", "tp"),
        P("seq", "tp"),
        P("tp", None),
        P(),
        P(),
        P(),
    )
    return jax.shard_map(
        per_device, mesh=mesh, in_specs=placed, out_specs=P("seq", "tp"), check_vma=False
    )
```
